32 devices in a mesh: groups: 2 (over y), leaf: 4 (over z), sub: 2 (over x), chan: 2 (over core).
Axes of the slice: x: 2, y: 2, z: 4, core: 2. Of those that a mesh axis runs over, the one named last changes fastest.
Arguments:
- charges: bfloat16 [2, 8, 32768], P('chan', None, ('groups', 'leaf', 'sub')), parts along dimension 2, may hold values from -6 to 6
- positions: float32 [3, 32768], P(None, ('groups', 'leaf', 'sub')), parts along dimension 1, may hold values from -6 to 6
- harmonics: bfloat16 [49, 32768], P(None, ('groups', 'leaf', 'sub')), parts along dimension 1, may hold values from -1.5 to 1.5
- operators: bfloat16 [316, 49, 49], replicated, may hold values from -0.0625 to 0.0625
- leaf_atoms: int32 [16, 64], P(('groups', 'leaf', 'sub')), parts along dimension 0, may hold values from 1 to 32, 1024 in all within a row
- near_lists: int32 [27, 1024], P(None, ('groups', 'leaf', 'sub')), parts along dimension 1, may hold values from 0 to 96, as said below
- requests: int32 [16, 8, 8], P(('groups', 'leaf', 'sub')), parts along dimension 0, may hold values from 0 to 63, as said below
- m2l_slots: int32 [316, 1024], P(None, ('groups', 'leaf', 'sub')), parts along dimension 1, may hold values from 0 to 128, as said below
Outputs:
- potentials: float32 [2, 8, 32768], P('chan', None, ('groups', 'leaf', 'sub')), parts along dimension 2
The draws below stay inside these ranges and needn't reach their ends.
There are 2 independent parts, one for each index of `groups`. The reference program is written for one: setup_inputs(seed, part) draws one part's arguments, and reference() takes and returns one part's arrays. A program takes and returns all parts, laid end to end along the dimension named above; an argument that names none is the same for every part. Nothing has to cross between parts.
Inputs may be any that keep to these rules, and one draw needn't show every extreme that they name: `leaf_atoms`: each device's 64 counts sum to 1024. `near_lists`: entries name distinct values within one leaf's list; 96 means none. `requests`: A device reads no leaves from itself; unused entries are 0. `m2l_slots`: 128 means none; slots of a device's own rank among the received blocks, and unused request entries, are never named.
All inputs are finite; a program needn't handle non-finite values.
Results may differ from the reference program's by a relative error of at most 0.0037.
Values may be sent and summed in bfloat16 or wider, within the bound.
A program may use at most 64 MiB of HBM per device.

```python
import math
import jax
import jax.numpy as jnp
import numpy as np
from jax import lax

TERMS = 49
CH = 8
NTYPE = 316
A_LEAF = 32
L_DEV = 64
CAP = 8
HALO = 16
NN = 27
NDEV = 8
LEAVES = 512
SLOTS = 128
ATOM_DEV = 1024


def plan_counts(key):
    key = jax.random.fold_in(key, 11)
    ranks = jnp.arange(NDEV, dtype=jnp.int32)
    lowest = max(CAP // 2, 1)
    counts = jax.random.randint(key, (NDEV, NDEV), lowest, CAP + 1)
    sibling = ranks + 1 - 2 * (ranks % 2)
    counts = counts.at[ranks, sibling].set(CAP)
    counts = jnp.where(ranks[:, None] == ranks[None, :], 0, counts)
    return counts.astype(jnp.int32)


def draw_requests(key, part):
    counts = plan_counts(key)
    key = jax.random.fold_in(key, 3)
    picks = jax.random.randint(key, (NDEV, NDEV, CAP), 0, L_DEV)
    used = jnp.arange(CAP)[None, None, :] < counts[:, :, None]
    return jnp.where(used, picks, 0).astype(jnp.int32)


def draw_m2l_slots(key, part):
    counts = plan_counts(key)
    key = jax.random.fold_in(key, 5)
    keys = jax.random.split(key, 6)
    shape = (NTYPE, NDEV, L_DEV)
    device_rank = jnp.broadcast_to(jnp.arange(NDEV)[None, :, None], shape)
    chosen = jax.random.randint(keys[1], shape, 0, 5) < 3
    local_pick = jax.random.randint(keys[2], shape, 0, L_DEV)
    is_local = jax.random.randint(keys[3], shape, 0, 2) == 0
    step_away = jax.random.randint(keys[4], shape, 0, NDEV - 1)
    peer_pick = (device_rank + 1 + step_away) % NDEV
    held = jnp.maximum(counts[device_rank, peer_pick], 1)
    slot_pick = jax.random.randint(keys[5], shape, 0, 64 * CAP) % held
    remote = L_DEV + peer_pick * CAP + slot_pick
    entry = jnp.where(chosen, jnp.where(is_local, local_pick, remote), SLOTS)
    type_rank = jnp.arange(NTYPE)[:, None, None]
    leaf_rank = jnp.arange(L_DEV)[None, None, :]
    flat = jnp.broadcast_to(type_rank // 3 * L_DEV + leaf_rank, shape)
    flat_peer = jnp.minimum(flat // CAP, NDEV - 1)
    placed = (flat < NDEV * CAP) & (flat % CAP < counts[device_rank, flat_peer])
    entry = jnp.where(placed, L_DEV + flat, entry)
    return entry.reshape(NTYPE, LEAVES).astype(jnp.int32)


def draw_near_lists(key, part):
    key = jax.random.fold_in(key, 7)
    key_order, key_kept = jax.random.split(key)
    window = 2 * HALO + 1
    scores = jax.random.randint(key_order, (LEAVES, window), 0, 1 << 20) * window + jnp.arange(window)[None, :]
    order = jnp.argsort(scores, axis=1)[:, :NN]
    leaf_rank = jnp.arange(LEAVES) % L_DEV
    entry = leaf_rank[:, None] + order
    kept = jax.random.randint(key_kept, (LEAVES, 1), NN - NN // 4, NN + 1)
    entry = jnp.where(jnp.arange(NN)[None, :] < kept, entry, L_DEV + 2 * HALO)
    return entry.T.astype(jnp.int32)


def level_of(rng, dims, cuts, low, high):
    loudness, own = 1.0, jax.random.fold_in(rng, 6)
    for position, blocks in cuts:
        heights = jnp.exp(jax.random.uniform(jax.random.fold_in(own, position), (blocks,), jnp.float32, low / len(cuts), high / len(cuts)))
        loudness = loudness * jnp.repeat(heights, dims[position] // blocks).reshape([-1 if axis == position else 1 for axis in range(len(dims))])
    return loudness


def split_up(number_of, total, reach, slope):
    loads = [(1 << 20) // math.isqrt(standing ** slope) + 1 for standing in range(2, number_of + 1)]
    spare, given = total - reach - (number_of - 1), [1] * (number_of - 1)
    while spare > 0:
        free = [i for i in range(number_of - 1) if given[i] < reach]
        mass, budget = sum([loads[i] for i in free]), spare
        for i in free:
            addition = min(reach - given[i], max(1, budget * loads[i] // mass), spare)
            given[i] = given[i] + addition
            spare = spare - addition
    return np.array([reach] + given)


def uneven(key, number_of, total, limit, lean):
    if number_of == 2:
        one = jax.random.randint(key, (), max(1, total - limit), min(limit, total - 1) + 1)
        return jnp.stack([one, total - one])
    tallies = jnp.asarray(split_up(number_of, total, limit, lean), jnp.int32)
    couples = (number_of - 1) // 2
    donor, taker = tallies[1:1 + 2 * couples:2], tallies[2:2 + 2 * couples:2]
    margin = jnp.minimum(donor - 1, limit - taker)
    passed = jax.random.randint(jax.random.fold_in(key, 1), (couples,), 0, 1 << 20) % (margin + 1)
    tallies = tallies.at[1:1 + 2 * couples:2].set(donor - passed).at[2:2 + 2 * couples:2].set(taker + passed)
    return tallies[jax.random.permutation(jax.random.fold_in(key, 2), number_of)]


def bell_draw(key, extent, scale, reach, shards=(), held_as=jnp.bfloat16):
    factor_of = level_of(key, extent, shards, -0.22, 0.18) if shards else 1.0
    drawn = jax.random.normal(key, extent, jnp.float32) * scale * factor_of
    return jnp.minimum(jnp.maximum(drawn, -reach), reach).astype(held_as)


def setup_inputs(seed: int = 0, part: int = 0) -> dict:
    arg_keys = jax.random.split(jax.random.key(seed), 9)
    own_keys = jax.random.split(jax.random.fold_in(arg_keys[8], part), 9)
    charges = bell_draw(own_keys[0], (2, CH, LEAVES * A_LEAF), 1.0, 6.0, ((0, 2), (2, 8)))
    positions = bell_draw(own_keys[1], (3, LEAVES * A_LEAF), 1.0, 6.0, ((1, 8),), jnp.float32)
    harmonics = bell_draw(own_keys[2], (TERMS, LEAVES * A_LEAF), (A_LEAF // 2) ** -0.5, 1.5, ((1, 8),))
    operators = bell_draw(arg_keys[3], (NTYPE, TERMS, TERMS), (TERMS * NTYPE * 3 // 5) ** -0.5, 0.0625)
    leaf_atoms = jax.vmap(lambda own: uneven(own, L_DEV, ATOM_DEV, A_LEAF, 2))(jax.random.split(own_keys[4], NDEV)).reshape((NDEV, L_DEV)).astype(jnp.int32)
    near_lists = draw_near_lists(jax.random.fold_in(jax.random.fold_in(arg_keys[8], part), 71), part)
    requests = draw_requests(jax.random.fold_in(jax.random.fold_in(arg_keys[8], part), 71), part)
    m2l_slots = draw_m2l_slots(jax.random.fold_in(jax.random.fold_in(arg_keys[8], part), 71), part)
    return {"charges": charges, "positions": positions, "harmonics": harmonics, "operators": operators, "leaf_atoms": leaf_atoms, "near_lists": near_lists, "requests": requests, "m2l_slots": m2l_slots}


SOFT_SQ = 0.0625
NEAR_GAIN = 0.1

def near_tile(targets, nbr_pos, nbr_charge):
    squared = sum(((targets[coordinate][None, :, :, None] - nbr_pos[coordinate][:, :, None, :]) ** 2 for coordinate in range(3)))
    kernel = lax.rsqrt(squared + SOFT_SQ).astype(jnp.bfloat16)
    return jnp.einsum('nlij,cnlj->cli', kernel.astype(jnp.float32), nbr_charge.astype(jnp.float32))

def reference(charges, positions, harmonics, operators, leaf_atoms, near_lists, requests, m2l_slots):
    alive = jnp.arange(A_LEAF)[None, :] < leaf_atoms.reshape(LEAVES)[:, None]
    alive_flat = alive.reshape(-1)
    masked = charges * alive_flat.astype(jnp.bfloat16)[None, None, :]
    harmonic_grid = harmonics.astype(jnp.float32).reshape(TERMS, LEAVES, A_LEAF)
    charge_grid = masked.astype(jnp.float32).reshape(2, CH, LEAVES, A_LEAF)
    moments = jnp.einsum('tla,fcla->fltc', harmonic_grid, charge_grid).astype(jnp.bfloat16)
    leaf_rank = jnp.arange(LEAVES, dtype=jnp.int32)
    device_rank = (leaf_rank // L_DEV)[None, :]
    remote = m2l_slots - L_DEV
    peer_rank = jnp.clip(remote // CAP, 0, NDEV - 1).astype(jnp.int32)
    slot_rank = (remote % CAP).astype(jnp.int32)
    asked_leaf = requests[jnp.broadcast_to(device_rank, m2l_slots.shape), peer_rank, slot_rank]
    source = jnp.where(m2l_slots < L_DEV, device_rank * L_DEV + m2l_slots, jnp.where(m2l_slots < SLOTS, peer_rank * L_DEV + asked_leaf, LEAVES)).astype(jnp.int32)
    padded = jnp.concatenate([moments, jnp.zeros((2, 1, TERMS, CH), jnp.bfloat16)], axis=1)

    def add_type(running, block_pair):
        table, operator = block_pair
        gathered = padded[:, table].astype(jnp.float32)
        return (running + jnp.einsum('uv,flvc->fluc', operator.astype(jnp.float32), gathered), None)
    start = jnp.zeros((2, LEAVES, TERMS, CH), jnp.float32)
    local_exp = lax.scan(add_type, start, (source, operators))[0].astype(jnp.bfloat16)
    far_field = jnp.einsum('tla,fltc->fcla', harmonic_grid, local_exp.astype(jnp.float32))
    position_grid = positions.reshape(3, LEAVES, A_LEAF)
    pos_padded = jnp.pad(position_grid, ((0, 0), (HALO, HALO + 1), (0, 0)))
    charge_padded = jnp.pad(masked.reshape(2 * CH, LEAVES, A_LEAF), ((0, 0), (HALO, HALO + 1), (0, 0)))
    neighbour = jnp.where(near_lists == L_DEV + 2 * HALO, LEAVES + 2 * HALO, device_rank * L_DEV + near_lists).astype(jnp.int32)
    target_blocks = position_grid.reshape(3, NDEV, L_DEV, A_LEAF).transpose(1, 0, 2, 3)
    table_blocks = neighbour.reshape(NN, NDEV, L_DEV).transpose(1, 0, 2)

    def near_device(block_pair):
        targets, table = block_pair
        return near_tile(targets, pos_padded[:, table], charge_padded[:, table])
    near_parts = lax.map(near_device, (target_blocks, table_blocks))
    near_field = NEAR_GAIN * near_parts.transpose(1, 0, 2, 3).reshape(2, CH, LEAVES, A_LEAF)
    total = (far_field + near_field) * alive.astype(jnp.float32)[None, None]
    return total.reshape(2, CH, LEAVES * A_LEAF)
```

```python
import functools
import math

import jax
import jax.numpy as jnp
from jax import lax
from jax.experimental import pallas as pl
from jax.experimental.pallas import tpu as pltpu
from jax.sharding import PartitionSpec as P

HALO = 16
SOFT_SQ = 0.0625
NEAR_GAIN = 0.1
HALF = 64
STEP_TYPES = 16
NT = (((1,), (1,)), ((), ()))
F32 = jnp.float32
BF16 = jnp.bfloat16


def lane_iota(shape):
    return lax.broadcasted_iota(jnp.int32, shape, len(shape) - 1)


def chunk_mask(counts_ref, j, slots):
    shape = (8, 8 * slots)
    offset = lane_iota(shape) - slots * lax.broadcasted_iota(jnp.int32, shape, 0)
    counts = counts_ref[8 * j : 8 * j + 8, :]
    return (offset >= 0) & (offset < counts)


def fill_harmonics(harm_ref, harm2_ref):
    terms = harm_ref.shape[0]
    harm2_ref[...] = jnp.zeros_like(harm2_ref)
    harm2_ref[0:terms, :] = harm_ref[...]
    harm2_ref[HALF : HALF + terms, :] = harm_ref[...]


def compute_moments(charges_ref, counts_ref, harm2_ref, live_ref, mom_ref, leaves, slots):
    channels = charges_ref.shape[0]
    width = 8 * slots
    for j in range(leaves // 8):
        mask = chunk_mask(counts_ref, j, slots)
        q = charges_ref[:, j * width : (j + 1) * width].astype(F32)
        spread = jnp.where(mask[None], q[:, None, :], 0.0)
        live_ref[:, j * width : (j + 1) * width] = jnp.sum(spread, axis=1)
        m = lax.dot_general(
            spread.reshape(channels * 8, width).astype(BF16),
            harm2_ref[:, j * width : (j + 1) * width],
            NT,
            preferred_element_type=F32,
        )
        low = lane_iota((8, 128)) < HALF
        for pair in range(channels // 2):
            mom_ref[8 * j : 8 * j + 8, 128 * pair : 128 * pair + 128] = jnp.where(
                low, m[16 * pair : 16 * pair + 8], m[16 * pair + 8 : 16 * pair + 16]
            )


def build_rolled(window, rolled_ref, first_block):
    for b in range(window.shape[1] // 128):
        block = window[:, 128 * b : 128 * b + 128]
        for r in range(4):
            rolled_ref[r, first_block + b] = block if r == 0 else pltpu.roll(block, 32 * r, 1)


def compute_near(near_ref, rolled_ref, pos_ref, out_ref, leaves, slots, neighbours):
    groups = -(-neighbours // 4)
    last = rolled_ref.shape[1] - 1
    lane = lane_iota((16, 128))

    def body(g, carry):
        columns = pl.ds(pl.multiple_of(g * 128, 128), 128)
        targets = jnp.transpose(pos_ref[:, columns])
        kernels, charges = [], []
        for leaf in range(4):
            tgt = targets[32 * leaf : 32 * leaf + 32]
            tgt = [jnp.broadcast_to(tgt[:, k : k + 1], (32, 128)) for k in range(3)]
            k_parts, q_parts = [], []
            for n4 in range(groups):
                src = None
                for j in range(4):
                    n = 4 * n4 + j
                    if n < neighbours:
                        e = near_ref[n, g * 4 + leaf]
                        piece = rolled_ref[(j + 4 - e % 4) % 4, e // 4]
                    else:
                        piece = rolled_ref[0, last]
                    src = piece if src is None else jnp.where(lane >= 32 * j, piece, src)
                squared = None
                for k in range(3):
                    d = tgt[k] - src[8 + k : 9 + k]
                    squared = d * d if squared is None else squared + d * d
                k_parts.append(lax.rsqrt(squared + SOFT_SQ).astype(BF16))
                q_parts.append(src[0:8])
            kernels.append(jnp.concatenate(k_parts, axis=1))
            charges.append(jnp.concatenate(q_parts, axis=1))
        kernels = jnp.concatenate(kernels, axis=0)
        charges = jnp.concatenate(charges, axis=0).astype(BF16)
        full = lax.dot_general(charges, kernels, NT, preferred_element_type=F32)
        lane8 = lane_iota((8, 128))
        near = full[0:8]
        for leaf in range(1, 4):
            near = jnp.where(lane8 >= 32 * leaf, full[8 * leaf : 8 * leaf + 8], near)
        out_ref[:, columns] = near
        return carry

    lax.fori_loop(0, leaves // 4, body, 0)


def build_table(first, rows, value, table_ref, slots_pad):
    low = lane_iota((rows, 128)) < HALF
    for pair in range(value.shape[1] // 128):
        p = value[:, 128 * pair : 128 * pair + 128]
        r = pltpu.roll(p, HALF, 1)
        c0, c1 = 256 * pair, 256 * pair + 128
        table_ref[first : first + rows, c0 : c0 + 128] = jnp.where(low, p, 0.0).astype(BF16)
        table_ref[first : first + rows, c1 : c1 + 128] = jnp.where(low, r, 0.0).astype(BF16)
        second = slots_pad + first
        table_ref[second : second + rows, c0 : c0 + 128] = jnp.where(low, 0.0, r).astype(BF16)
        table_ref[second : second + rows, c1 : c1 + 128] = jnp.where(low, 0.0, p).astype(BF16)


def compute_local(index_ref, op_ref, table_ref, gathered_ref, acc_ref, leaves, channels):
    slots_pad = table_ref.shape[0] // 2
    pairs = STEP_TYPES // 2
    depth = STEP_TYPES * HALF
    acc_ref[...] = jnp.zeros_like(acc_ref)

    def body(step, carry):
        index = index_ref[step]
        lane = lane_iota((leaves, slots_pad))
        hot = []
        for pair in range(pairs):
            hot.append(
                jnp.concatenate(
                    [
                        jnp.where(index[:, t : t + 1] == lane, 1.0, 0.0).astype(BF16)
                        for t in (2 * pair, 2 * pair + 1)
                    ],
                    axis=1,
                )
            )
        hot = jnp.concatenate(hot, axis=0)
        for c2 in range(channels // 2):
            got = jnp.dot(
                hot, table_ref[:, 256 * c2 : 256 * c2 + 256], preferred_element_type=F32
            ).astype(BF16)
            for half in range(2):
                row = (2 * c2 + half) * leaves
                for pair in range(pairs):
                    gathered_ref[row : row + leaves, 128 * pair : 128 * pair + 128] = got[
                        leaves * pair : leaves * pair + leaves, 128 * half : 128 * half + 128
                    ]
        rows = pl.ds(pl.multiple_of(step * depth, depth), depth)
        acc_ref[...] += jnp.dot(gathered_ref[...], op_ref[rows, :], preferred_element_type=F32)
        return carry

    lax.fori_loop(0, index_ref.shape[0], body, 0)


def finish(acc_ref, harm2_ref, counts_ref, near_ref, out_ref, leaves, slots, channels):
    width = 8 * slots
    for j in range(leaves // 8):
        local = jnp.concatenate(
            [acc_ref[c * leaves + 8 * j : c * leaves + 8 * j + 8] for c in range(channels)], axis=0
        ).astype(BF16)
        columns = slice(j * width, (j + 1) * width)
        far = jnp.dot(local, harm2_ref[:, columns], preferred_element_type=F32)
        mask = chunk_mask(counts_ref, j, slots)
        far = jnp.sum(jnp.where(mask[None], far.reshape(channels, 8, width), 0.0), axis=1)
        alive = jnp.sum(jnp.where(mask, 1.0, 0.0), axis=0, keepdims=True)
        out_ref[:, columns] = far + (NEAR_GAIN * alive) * near_ref[:, columns]


def moments_kernel(dims, charges_ref, counts_ref, harm_ref, mom_ref, live_ref, harm2_ref, scratch):
    leaves, slots = dims
    fill_harmonics(harm_ref, harm2_ref)
    compute_moments(charges_ref, counts_ref, harm2_ref, live_ref, scratch, leaves, slots)
    mom_ref[...] = scratch[...].astype(BF16)


def main_kernel(
    dims, near_lists_ref, index_ref, op_ref, mom_ref, got_ref, window_ref, pos_ref, counts_ref,
    harm_ref, out_ref, harm2_ref, rolled_ref, near_ref, table_ref, gathered_ref, acc_ref,
):
    leaves, slots, channels, neighbours = dims
    fill_harmonics(harm_ref, harm2_ref)
    rolled_ref[:, rolled_ref.shape[1] - 1] = jnp.zeros((4, 16, 128), F32)
    build_rolled(window_ref[...], rolled_ref, 0)
    compute_near(near_lists_ref, rolled_ref, pos_ref, near_ref, leaves, slots, neighbours)
    slots_pad = table_ref.shape[0] // 2
    filled = leaves + got_ref.shape[0]
    if filled < slots_pad:
        for base in (0, slots_pad):
            table_ref[base + filled : base + slots_pad, :] = jnp.zeros(
                (slots_pad - filled, table_ref.shape[1]), BF16
            )
    build_table(0, leaves, mom_ref[...].astype(F32), table_ref, slots_pad)
    build_table(leaves, got_ref.shape[0], got_ref[...].astype(F32), table_ref, slots_pad)
    compute_local(index_ref, op_ref, table_ref, gathered_ref, acc_ref, leaves, channels)
    finish(acc_ref, harm2_ref, counts_ref, near_ref, out_ref, leaves, slots, channels)


def per_device(
    charges, positions, harmonics, operators, leaf_atoms, near_lists, requests, m2l_slots
):
    leaves = leaf_atoms.shape[1]
    atoms = positions.shape[1]
    slots = atoms // leaves
    terms = harmonics.shape[0]
    channels = charges.shape[1]
    types = operators.shape[0]
    neighbours = near_lists.shape[0]
    fetched = requests.shape[1] * requests.shape[2]
    slots_pad = -(-(leaves + fetched) // 128) * 128
    steps = -(-types // STEP_TYPES)
    types_pad = steps * STEP_TYPES
    counts = leaf_atoms.reshape(leaves, 1)
    vmem = pl.BlockSpec(memory_space=pltpu.VMEM)
    smem = pl.BlockSpec(memory_space=pltpu.SMEM)
    params = pltpu.CompilerParams(vmem_limit_bytes=48 * 1024 * 1024)

    moments, live = pl.pallas_call(
        functools.partial(moments_kernel, (leaves, slots)),
        out_shape=(
            jax.ShapeDtypeStruct((leaves, channels * HALF), BF16),
            jax.ShapeDtypeStruct((channels, atoms), F32),
        ),
        in_specs=[vmem] * 3,
        out_specs=(vmem, vmem),
        scratch_shapes=[pltpu.VMEM((128, atoms), BF16), pltpu.VMEM((leaves, channels * HALF), F32)],
        compiler_params=params,
    )(charges[0], counts, harmonics)

    axes = ("leaf", "sub")
    asked = lax.all_to_all(requests[0], axes, split_axis=0, concat_axis=0, tiled=True)
    got = lax.all_to_all(moments[asked], axes, split_axis=0, concat_axis=0, tiled=True)
    got = got.reshape(fetched, channels * HALF)
    stacked = jnp.concatenate(
        [live, positions, jnp.zeros((16 - channels - 3, atoms), F32)], axis=0
    )
    count = lax.axis_size(axes)
    forward = [(i, i + 1) for i in range(count - 1)]
    backward = [(t, s) for s, t in forward]
    width = HALO * slots
    low = lax.ppermute(stacked[:, atoms - width :], axes, forward)
    high = lax.ppermute(stacked[:, :width], axes, backward)
    window = jnp.concatenate([low, stacked, high], axis=1)
    index = jnp.pad(m2l_slots, ((0, types_pad - types), (0, 0)), constant_values=slots_pad)
    index = index.reshape(steps, STEP_TYPES, leaves).transpose(0, 2, 1)
    ops = jnp.pad(
        operators.transpose(0, 2, 1),
        ((0, types_pad - types), (0, HALF - terms), (0, 128 - terms)),
    ).reshape(types_pad * HALF, 128)

    pos8 = jnp.pad(positions, ((0, 5), (0, 0)))
    out = pl.pallas_call(
        functools.partial(main_kernel, (leaves, slots, channels, neighbours)),
        out_shape=jax.ShapeDtypeStruct((channels, atoms), F32),
        in_specs=[smem] + [vmem] * 8,
        out_specs=vmem,
        scratch_shapes=[
            pltpu.VMEM((128, atoms), BF16),
            pltpu.VMEM((4, window.shape[1] // 128 + 1, 16, 128), F32),
            pltpu.VMEM((channels, atoms), F32),
            pltpu.VMEM((2 * slots_pad, channels * 128), BF16),
            pltpu.VMEM((channels * leaves, STEP_TYPES * HALF), BF16),
            pltpu.VMEM((channels * leaves, 128), F32),
        ],
        compiler_params=params,
    )(near_lists, index, ops, moments, got, window, pos8, counts, harmonics)
    return out[None]


def solution(mesh):
    return jax.shard_map(
        per_device,
        mesh=mesh,
        in_specs=(
            P("chan", None, ("groups", "leaf", "sub")),
            P(None, ("groups", "leaf", "sub")),
            P(None, ("groups", "leaf", "sub")),
            P(),
            P(("groups", "leaf", "sub"), None),
            P(None, ("groups", "leaf", "sub")),
            P(("groups", "leaf", "sub"), None, None),
            P(None, ("groups", "leaf", "sub")),
        ),
        out_specs=P("chan", None, ("groups", "leaf", "sub")),
        check_vma=False,
    )
```

```python
import functools
import math

import jax
import jax.numpy as jnp
from jax import lax
from jax.experimental import pallas as pl
from jax.experimental.pallas import tpu as pltpu
from jax.sharding import PartitionSpec as P

HALO = 16
SOFT_SQ = 0.0625
NEAR_GAIN = 0.1
HALF = 64
NT = (((1,), (1,)), ((), ()))
F32 = jnp.float32
BF16 = jnp.bfloat16


def lane_iota(shape):
    return lax.broadcasted_iota(jnp.int32, shape, len(shape) - 1)


def chunk_mask(counts_ref, j, slots):
    shape = (8, 8 * slots)
    offset = lane_iota(shape) - slots * lax.broadcasted_iota(jnp.int32, shape, 0)
    counts = counts_ref[8 * j : 8 * j + 8, :]
    return (offset >= 0) & (offset < counts)


def fill_harmonics(harm_ref, harm2_ref):
    terms = harm_ref.shape[0]
    harm2_ref[...] = jnp.zeros_like(harm2_ref)
    harm2_ref[0:terms, :] = harm_ref[...]
    harm2_ref[HALF : HALF + terms, :] = harm_ref[...]


def compute_moments(charges_ref, counts_ref, harm2_ref, live_ref, mom_ref, leaves, slots):
    channels = charges_ref.shape[0]
    width = 8 * slots
    for j in range(leaves // 8):
        mask = chunk_mask(counts_ref, j, slots)
        q = charges_ref[:, j * width : (j + 1) * width].astype(F32)
        spread = jnp.where(mask[None], q[:, None, :], 0.0)
        live_ref[:, j * width : (j + 1) * width] = jnp.sum(spread, axis=1)
        m = lax.dot_general(
            spread.reshape(channels * 8, width).astype(BF16),
            harm2_ref[:, j * width : (j + 1) * width],
            NT,
            preferred_element_type=F32,
        )
        low = lane_iota((8, 128)) < HALF
        for pair in range(channels // 2):
            mom_ref[8 * j : 8 * j + 8, 128 * pair : 128 * pair + 128] = jnp.where(
                low, m[16 * pair : 16 * pair + 8], m[16 * pair + 8 : 16 * pair + 16]
            )


def build_rolled(window, rolled_ref, first_block):
    for b in range(window.shape[1] // 128):
        block = window[:, 128 * b : 128 * b + 128]
        for r in range(4):
            rolled_ref[r, first_block + b] = block if r == 0 else pltpu.roll(block, 32 * r, 1)


def compute_near(near_ref, rolled_ref, pos_ref, out_ref, leaves, slots, neighbours):
    groups = -(-neighbours // 4)
    last = rolled_ref.shape[1] - 1
    lane = lane_iota((16, 128))

    def body(g, carry):
        columns = pl.ds(pl.multiple_of(g * 128, 128), 128)
        targets = jnp.transpose(pos_ref[:, columns])
        kernels, charges = [], []
        for leaf in range(4):
            tgt = targets[32 * leaf : 32 * leaf + 32]
            tgt = [jnp.broadcast_to(tgt[:, k : k + 1], (32, 128)) for k in range(3)]
            k_parts, q_parts = [], []
            for n4 in range(groups):
                src = None
                for j in range(4):
                    n = 4 * n4 + j
                    if n < neighbours:
                        e = near_ref[n, g * 4 + leaf]
                        piece = rolled_ref[(j + 4 - e % 4) % 4, e // 4]
                    else:
                        piece = rolled_ref[0, last]
                    src = piece if src is None else jnp.where(lane >= 32 * j, piece, src)
                squared = None
                for k in range(3):
                    d = tgt[k] - src[8 + k : 9 + k]
                    squared = d * d if squared is None else squared + d * d
                k_parts.append(lax.rsqrt(squared + SOFT_SQ).astype(BF16))
                q_parts.append(src[0:8])
            kernels.append(jnp.concatenate(k_parts, axis=1))
            charges.append(jnp.concatenate(q_parts, axis=1))
        kernels = jnp.concatenate(kernels, axis=0)
        charges = jnp.concatenate(charges, axis=0).astype(BF16)
        full = lax.dot_general(charges, kernels, NT, preferred_element_type=F32)
        lane8 = lane_iota((8, 128))
        near = full[0:8]
        for leaf in range(1, 4):
            near = jnp.where(lane8 >= 32 * leaf, full[8 * leaf : 8 * leaf + 8], near)
        out_ref[:, columns] = near
        return carry

    lax.fori_loop(0, leaves // 4, body, 0)


def gather_lanes(row, index):
    return jnp.take_along_axis(row, index, axis=1, mode="promise_in_bounds")


def compute_local(index_ref, op_ref, table_ref, acc_ref, leaves, channels):
    terms, _, types_pad = op_ref.shape
    blocks = table_ref.shape[0]
    batch = math.gcd(terms, 7)
    acc_ref[...] = jnp.zeros_like(acc_ref)

    def body(step, carry):
        parts = []
        for k in range(batch):
            v = step * batch + k
            rows = []
            for c in range(channels):
                lines = [
                    jnp.broadcast_to(table_ref[b, pl.ds(c * HALF + v, 1), :], (8, 128))
                    for b in range(blocks)
                ]
                for l8 in range(leaves // 8):
                    columns = []
                    for t in range(types_pad // 128):
                        index = index_ref[8 * l8 : 8 * l8 + 8, 128 * t : 128 * t + 128]
                        if blocks == 1:
                            got = gather_lanes(lines[0], index)
                        else:
                            got = jnp.zeros((8, 128), F32)
                            for b in range(blocks):
                                piece = gather_lanes(lines[b], index % 128)
                                got = jnp.where(index // 128 == b, piece, got)
                        columns.append(got)
                    rows.append(jnp.concatenate(columns, axis=1))
            parts.append(jnp.concatenate(rows, axis=0).astype(BF16))
        sources = jnp.concatenate(parts, axis=1)
        ops = jnp.concatenate([op_ref[step * batch + k] for k in range(batch)], axis=1)
        acc_ref[...] += lax.dot_general(sources, ops, NT, preferred_element_type=F32)
        return carry

    lax.fori_loop(0, terms // batch, body, 0)


def finish(acc_ref, harm2_ref, counts_ref, near_ref, out_ref, leaves, slots, channels):
    width = 8 * slots
    for j in range(leaves // 8):
        local = jnp.concatenate(
            [acc_ref[c * leaves + 8 * j : c * leaves + 8 * j + 8] for c in range(channels)], axis=0
        ).astype(BF16)
        columns = slice(j * width, (j + 1) * width)
        far = jnp.dot(local, harm2_ref[0:HALF, columns], preferred_element_type=F32)
        mask = chunk_mask(counts_ref, j, slots)
        far = jnp.sum(jnp.where(mask[None], far.reshape(channels, 8, width), 0.0), axis=1)
        alive = jnp.sum(jnp.where(mask, 1.0, 0.0), axis=0, keepdims=True)
        out_ref[:, columns] = far + (NEAR_GAIN * alive) * near_ref[:, columns]


def moments_kernel(dims, charges_ref, counts_ref, harm_ref, mom_ref, live_ref, harm2_ref, scratch):
    leaves, slots = dims
    fill_harmonics(harm_ref, harm2_ref)
    compute_moments(charges_ref, counts_ref, harm2_ref, live_ref, scratch, leaves, slots)
    mom_ref[...] = scratch[...].astype(BF16)


def near_kernel(dims, near_lists_ref, window_ref, pos_ref, near_ref, rolled_ref):
    leaves, slots, channels, neighbours = dims
    rolled_ref[:, rolled_ref.shape[1] - 1] = jnp.zeros((4, 16, 128), F32)
    build_rolled(window_ref[...], rolled_ref, 0)
    compute_near(near_lists_ref, rolled_ref, pos_ref, near_ref, leaves, slots, neighbours)


def far_kernel(
    dims, index_ref, op_ref, sources_ref, near_ref, counts_ref, harm_ref, out_ref, harm2_ref,
    table_ref, acc_ref,
):
    leaves, slots, channels = dims
    fill_harmonics(harm_ref, harm2_ref)
    for b in range(table_ref.shape[0]):
        block = sources_ref[128 * b : 128 * b + 128, :].astype(F32)
        for p in range(block.shape[1] // 128):
            table_ref[b, 128 * p : 128 * p + 128, :] = jnp.transpose(
                block[:, 128 * p : 128 * p + 128]
            )
    compute_local(index_ref, op_ref, table_ref, acc_ref, leaves, channels)
    finish(acc_ref, harm2_ref, counts_ref, near_ref, out_ref, leaves, slots, channels)


def per_device(
    charges, positions, harmonics, operators, leaf_atoms, near_lists, requests, m2l_slots
):
    leaves = leaf_atoms.shape[1]
    atoms = positions.shape[1]
    slots = atoms // leaves
    terms = harmonics.shape[0]
    channels = charges.shape[1]
    types = operators.shape[0]
    neighbours = near_lists.shape[0]
    fetched = requests.shape[1] * requests.shape[2]
    slots_pad = -(-(leaves + fetched) // 128) * 128
    types_pad = -(-types // 128) * 128
    counts = leaf_atoms.reshape(leaves, 1)
    vmem = pl.BlockSpec(memory_space=pltpu.VMEM)
    smem = pl.BlockSpec(memory_space=pltpu.SMEM)
    params = pltpu.CompilerParams(vmem_limit_bytes=48 * 1024 * 1024)

    moments, live = pl.pallas_call(
        functools.partial(moments_kernel, (leaves, slots)),
        out_shape=(
            jax.ShapeDtypeStruct((leaves, channels * HALF), BF16),
            jax.ShapeDtypeStruct((channels, atoms), F32),
        ),
        in_specs=[vmem] * 3,
        out_specs=(vmem, vmem),
        scratch_shapes=[pltpu.VMEM((128, atoms), BF16), pltpu.VMEM((leaves, channels * HALF), F32)],
        compiler_params=params,
    )(charges[0], counts, harmonics)

    axes = ("leaf", "sub")
    asked = lax.all_to_all(requests[0], axes, split_axis=0, concat_axis=0, tiled=True)
    got = lax.all_to_all(moments[asked], axes, split_axis=0, concat_axis=0, tiled=True)
    got = got.reshape(fetched, channels * HALF)
    stacked = jnp.concatenate(
        [live, positions, jnp.zeros((16 - channels - 3, atoms), F32)], axis=0
    )
    count = lax.axis_size(axes)
    forward = [(i, i + 1) for i in range(count - 1)]
    backward = [(t, s) for s, t in forward]
    width = HALO * slots
    low = lax.ppermute(stacked[:, atoms - width :], axes, forward)
    high = lax.ppermute(stacked[:, :width], axes, backward)
    window = jnp.concatenate([low, stacked, high], axis=1)
    me = lax.axis_index(axes)
    capacity = requests.shape[2]
    spare = leaves + capacity * me
    index = jnp.where(m2l_slots < leaves + fetched, m2l_slots, spare).T
    index = jnp.pad(index, ((0, 0), (0, types_pad - types)))
    ops = jnp.pad(
        operators.transpose(2, 1, 0), ((0, 0), (0, HALF - terms), (0, types_pad - types))
    )
    own = jnp.arange(fetched)[:, None] // capacity == me
    sources = jnp.concatenate(
        [
            moments,
            jnp.where(own, 0, got),
            jnp.zeros((slots_pad - leaves - fetched, channels * HALF), BF16),
        ],
        axis=0,
    )
    pos8 = jnp.pad(positions, ((0, 5), (0, 0)))
    near = pl.pallas_call(
        functools.partial(near_kernel, (leaves, slots, channels, neighbours)),
        out_shape=jax.ShapeDtypeStruct((channels, atoms), F32),
        in_specs=[smem] + [vmem] * 2,
        out_specs=vmem,
        scratch_shapes=[pltpu.VMEM((4, window.shape[1] // 128 + 1, 16, 128), F32)],
        compiler_params=params,
    )(near_lists, window, pos8)
    out = pl.pallas_call(
        functools.partial(far_kernel, (leaves, slots, channels)),
        out_shape=jax.ShapeDtypeStruct((channels, atoms), F32),
        in_specs=[vmem] * 6,
        out_specs=vmem,
        scratch_shapes=[
            pltpu.VMEM((128, atoms), BF16),
            pltpu.VMEM((slots_pad // 128, channels * HALF, 128), F32),
            pltpu.VMEM((channels * leaves, HALF), F32),
        ],
        compiler_params=params,
    )(index, ops, sources, near, counts, harmonics)
    return out[None]


def solution(mesh):
    return jax.shard_map(
        per_device,
        mesh=mesh,
        in_specs=(
            P("chan", None, ("groups", "leaf", "sub")),
            P(None, ("groups", "leaf", "sub")),
            P(None, ("groups", "leaf", "sub")),
            P(),
            P(("groups", "leaf", "sub"), None),
            P(None, ("groups", "leaf", "sub")),
            P(("groups", "leaf", "sub"), None, None),
            P(None, ("groups", "leaf", "sub")),
        ),
        out_specs=P("chan", None, ("groups", "leaf", "sub")),
        check_vma=False,
    )
```

```python
import functools
import math

import jax
import jax.numpy as jnp
from jax import lax
from jax.experimental import pallas as pl
from jax.experimental.pallas import tpu as pltpu
from jax.sharding import PartitionSpec as P

HALO = 16
SOFT_SQ = 0.0625
NEAR_GAIN = 0.1
HALF = 64
NT = (((1,), (1,)), ((), ()))
F32 = jnp.float32
BF16 = jnp.bfloat16


def lane_iota(shape):
    return lax.broadcasted_iota(jnp.int32, shape, len(shape) - 1)


def chunk_mask(counts_ref, j, slots):
    shape = (8, 8 * slots)
    offset = lane_iota(shape) - slots * lax.broadcasted_iota(jnp.int32, shape, 0)
    counts = counts_ref[8 * j : 8 * j + 8, :]
    return (offset >= 0) & (offset < counts)


def fill_harmonics(harm_ref, harm2_ref):
    terms = harm_ref.shape[0]
    harm2_ref[...] = jnp.zeros_like(harm2_ref)
    harm2_ref[0:terms, :] = harm_ref[...]
    harm2_ref[HALF : HALF + terms, :] = harm_ref[...]


def compute_moments(charges_ref, counts_ref, harm2_ref, live_ref, mom_ref, leaves, slots):
    channels = charges_ref.shape[0]
    width = 8 * slots
    for j in range(leaves // 8):
        mask = chunk_mask(counts_ref, j, slots)
        q = charges_ref[:, j * width : (j + 1) * width].astype(F32)
        spread = jnp.where(mask[None], q[:, None, :], 0.0)
        live_ref[0:channels, j * width : (j + 1) * width] = jnp.sum(spread, axis=1)
        m = lax.dot_general(
            spread.reshape(channels * 8, width).astype(BF16),
            harm2_ref[:, j * width : (j + 1) * width],
            NT,
            preferred_element_type=F32,
        )
        low = lane_iota((8, 128)) < HALF
        for pair in range(channels // 2):
            mom_ref[8 * j : 8 * j + 8, 128 * pair : 128 * pair + 128] = jnp.where(
                low, m[16 * pair : 16 * pair + 8], m[16 * pair + 8 : 16 * pair + 16]
            )


def build_rolled(window, rolled_ref, first_block):
    for b in range(window.shape[1] // 128):
        block = window[:, 128 * b : 128 * b + 128]
        for r in range(4):
            rolled_ref[4 * (first_block + b) + r] = block if r == 0 else pltpu.roll(block, 32 * r, 1)


def compute_near(near_ref, rolled_ref, pos_ref, out_ref, leaves, slots, neighbours):
    groups = -(-neighbours // 4)
    last = rolled_ref.shape[0] - 1
    lane = lane_iota((16, 128))

    def body(g, carry):
        columns = pl.ds(pl.multiple_of(g * 128, 128), 128)
        targets = jnp.transpose(pos_ref[8:16, columns])
        kernels, charges = [], []
        for leaf in range(4):
            tgt = targets[32 * leaf : 32 * leaf + 32]
            tgt = [jnp.broadcast_to(tgt[:, k : k + 1], (32, 128)) for k in range(3)]
            k_parts, q_parts = [], []
            for n4 in range(groups):
                src = None
                for j in range(4):
                    n = 4 * n4 + j
                    if n < neighbours:
                        piece = rolled_ref[near_ref[n, g * 4 + leaf]]
                    else:
                        piece = rolled_ref[last]
                    src = piece if src is None else jnp.where(lane >= 32 * j, piece, src)
                squared = None
                for k in range(3):
                    d = tgt[k] - src[8 + k : 9 + k]
                    squared = d * d if squared is None else squared + d * d
                k_parts.append(lax.rsqrt(squared + SOFT_SQ).astype(BF16))
                q_parts.append(src[0:8])
            kernels.append(jnp.concatenate(k_parts, axis=1))
            charges.append(jnp.concatenate(q_parts, axis=1))
        kernels = jnp.concatenate(kernels, axis=0)
        charges = jnp.concatenate(charges, axis=0).astype(BF16)
        full = lax.dot_general(charges, kernels, NT, preferred_element_type=F32)
        lane8 = lane_iota((8, 128))
        near = full[0:8]
        for leaf in range(1, 4):
            near = jnp.where(lane8 >= 32 * leaf, full[8 * leaf : 8 * leaf + 8], near)
        out_ref[:, columns] = near
        return carry

    lax.fori_loop(0, leaves // 4, body, 0)


def gather_lanes(row, index):
    return jnp.take_along_axis(row, index, axis=1, mode="promise_in_bounds")


def compute_local(index_ref, op_ref, table_ref, acc_ref, leaves, channels):
    terms, _, types_pad = op_ref.shape
    blocks = table_ref.shape[0]
    batch = math.gcd(terms, 7)
    acc_ref[...] = jnp.zeros_like(acc_ref)

    def body(step, carry):
        parts = []
        for k in range(batch):
            v = step * batch + k
            rows = []
            for c in range(channels):
                lines = [
                    jnp.broadcast_to(table_ref[b, pl.ds(c * HALF + v, 1), :], (8, 128))
                    for b in range(blocks)
                ]
                for l8 in range(leaves // 8):
                    columns = []
                    for t in range(types_pad // 128):
                        index = index_ref[8 * l8 : 8 * l8 + 8, 128 * t : 128 * t + 128]
                        if blocks == 1:
                            got = gather_lanes(lines[0], index)
                        else:
                            got = jnp.zeros((8, 128), F32)
                            for b in range(blocks):
                                piece = gather_lanes(lines[b], index % 128)
                                got = jnp.where(index // 128 == b, piece, got)
                        columns.append(got)
                    rows.append(jnp.concatenate(columns, axis=1))
            parts.append(jnp.concatenate(rows, axis=0).astype(BF16))
        sources = jnp.concatenate(parts, axis=1)
        ops = jnp.concatenate([op_ref[step * batch + k] for k in range(batch)], axis=1)
        acc_ref[...] += lax.dot_general(sources, ops, NT, preferred_element_type=F32)
        return carry

    lax.fori_loop(0, terms // batch, body, 0)


def finish(acc_ref, harm2_ref, counts_ref, near_ref, out_ref, leaves, slots, channels):
    width = 8 * slots
    for j in range(leaves // 8):
        local = jnp.concatenate(
            [acc_ref[c * leaves + 8 * j : c * leaves + 8 * j + 8] for c in range(channels)], axis=0
        ).astype(BF16)
        columns = slice(j * width, (j + 1) * width)
        far = jnp.dot(local, harm2_ref[0:HALF, columns], preferred_element_type=F32)
        mask = chunk_mask(counts_ref, j, slots)
        far = jnp.sum(jnp.where(mask[None], far.reshape(channels, 8, width), 0.0), axis=1)
        alive = jnp.sum(jnp.where(mask, 1.0, 0.0), axis=0, keepdims=True)
        out_ref[:, columns] = far + (NEAR_GAIN * alive) * near_ref[:, columns]


def exchange_kernel(
    dims, near_index_ref, charges_ref, counts_ref, harm_ref, requests_ref, positions_ref,
    sources_ref, near_ref, harm2_ref, stacked_ref, moments_ref, rolled_ref, wanted_ref, asked_ref,
    reply_ref, got_ref, halo_ref, halo_send, halo_recv, ask_send, ask_recv, reply_send, reply_recv,
):
    leaves, slots, channels, neighbours, count, subs = dims
    capacity = requests_ref.shape[0]
    atoms = leaves * slots
    width = HALO * slots
    me = lax.axis_index("leaf") * subs + lax.axis_index("sub")

    def device(rank):
        return (lax.axis_index("groups"), rank // subs, rank % subs, lax.axis_index("chan"))

    def peer(offset):
        return (me + offset) % count

    barrier = pltpu.get_barrier_semaphore()
    for d in range(1, count):
        pl.semaphore_signal(
            barrier, inc=1, device_id=device(peer(d)), device_id_type=pl.DeviceIdType.MESH
        )

    for p in range(count):
        wanted_ref[p] = jnp.broadcast_to(requests_ref[:, p : p + 1], (capacity, 128))
    fill_harmonics(harm_ref, harm2_ref)
    stacked_ref[8:16, :] = jnp.zeros((8, atoms), F32)
    stacked_ref[8:11, :] = positions_ref[...]
    compute_moments(
        charges_ref, counts_ref, harm2_ref, stacked_ref, moments_ref, leaves, slots
    )
    pl.semaphore_wait(barrier, count - 1)

    def remote(src, dst, send, recv, rank):
        return pltpu.make_async_remote_copy(
            src_ref=src, dst_ref=dst, send_sem=send, recv_sem=recv, device_id=device(rank),
            device_id_type=pl.DeviceIdType.MESH,
        )

    asks = []
    for d in range(1, count):
        copy = remote(
            wanted_ref.at[peer(d)], asked_ref.at[d - 1], ask_send.at[d - 1], ask_recv.at[d - 1],
            peer(d),
        )
        copy.start()
        asks.append(copy)
    halos = [
        remote(
            stacked_ref.at[:, pl.ds(atoms - width, width)], halo_ref.at[0], halo_send.at[0],
            halo_recv.at[0], peer(1),
        ),
        remote(
            stacked_ref.at[:, pl.ds(0, width)], halo_ref.at[1], halo_send.at[1], halo_recv.at[1],
            peer(count - 1),
        ),
    ]
    for copy in halos:
        copy.start()

    moments = moments_ref[...].astype(BF16)
    build_rolled(stacked_ref[...], rolled_ref, width // 128)
    for r in range(4):
        rolled_ref[rolled_ref.shape[0] - 4 + r] = jnp.zeros((16, 128), F32)

    lane = lane_iota((capacity, leaves))
    for copy in asks:
        copy.wait_recv()
    hot = jnp.concatenate(
        [jnp.where(asked_ref[d - 1][:, :leaves] == lane, 1.0, 0.0) for d in range(1, count)],
        axis=0,
    ).astype(BF16)
    picked = jnp.dot(hot, moments, preferred_element_type=F32)
    half = channels * HALF // 2
    replies = []
    for d in range(1, count):
        block = picked[capacity * (d - 1) : capacity * d]
        reply_ref[d - 1] = jnp.concatenate([block[:, :half], block[:, half:]], axis=0).astype(BF16)
        copy = remote(
            reply_ref.at[d - 1], got_ref.at[d - 1], reply_send.at[d - 1], reply_recv.at[d - 1],
            peer(count - d),
        )
        copy.start()
        replies.append(copy)

    for copy in halos:
        copy.wait_recv()
    build_rolled(jnp.where(me == 0, 0.0, halo_ref[0]), rolled_ref, 0)
    build_rolled(
        jnp.where(me == count - 1, 0.0, halo_ref[1]), rolled_ref, (width + atoms) // 128
    )
    compute_near(near_index_ref, rolled_ref, stacked_ref, near_ref, leaves, slots, neighbours)

    sources_ref[0:leaves, :] = moments.astype(F32)
    sources_ref[leaves:, :] = jnp.zeros((sources_ref.shape[0] - leaves, channels * HALF), F32)
    for d in range(1, count):
        replies[d - 1].wait_recv()
        block = got_ref[d - 1].astype(F32)
        rows = pl.ds(pl.multiple_of(leaves + capacity * peer(d), 8), capacity)
        sources_ref[rows, 0:half] = block[0:capacity]
        sources_ref[rows, half : 2 * half] = block[capacity : 2 * capacity]
    for copy in asks + halos + replies:
        copy.wait_send()


def far_kernel(
    dims, index_ref, op_ref, sources_ref, near_ref, counts_ref, harm_ref, out_ref, harm2_ref,
    table_ref, acc_ref,
):
    leaves, slots, channels = dims
    fill_harmonics(harm_ref, harm2_ref)
    for b in range(table_ref.shape[0]):
        block = sources_ref[128 * b : 128 * b + 128, :]
        for p in range(block.shape[1] // 128):
            table_ref[b, 128 * p : 128 * p + 128, :] = jnp.transpose(
                block[:, 128 * p : 128 * p + 128]
            )
    compute_local(index_ref, op_ref, table_ref, acc_ref, leaves, channels)
    finish(acc_ref, harm2_ref, counts_ref, near_ref, out_ref, leaves, slots, channels)


def per_device(
    charges, positions, harmonics, operators, leaf_atoms, near_lists, requests, m2l_slots
):
    leaves = leaf_atoms.shape[1]
    atoms = positions.shape[1]
    slots = atoms // leaves
    terms = harmonics.shape[0]
    channels = charges.shape[1]
    types = operators.shape[0]
    neighbours = near_lists.shape[0]
    fetched = requests.shape[1] * requests.shape[2]
    slots_pad = -(-(leaves + fetched) // 128) * 128
    types_pad = -(-types // 128) * 128
    counts = leaf_atoms.reshape(leaves, 1)
    vmem = pl.BlockSpec(memory_space=pltpu.VMEM)
    smem = pl.BlockSpec(memory_space=pltpu.SMEM)
    params = pltpu.CompilerParams(vmem_limit_bytes=48 * 1024 * 1024)
    axes = ("leaf", "sub")
    count = requests.shape[1]
    capacity = requests.shape[2]
    window_blocks = (leaves + 2 * HALO) * slots // 128
    width = HALO * slots
    peers = max(count - 1, 1)
    turn = (jnp.arange(neighbours, dtype=jnp.int32)[:, None] - near_lists) & 3
    near_index = (near_lists & ~3) + turn
    dma = pltpu.SemaphoreType.DMA
    sources, near = pl.pallas_call(
        functools.partial(
            exchange_kernel,
            (leaves, slots, channels, neighbours, count, lax.axis_size("sub")),
        ),
        out_shape=(
            jax.ShapeDtypeStruct((slots_pad, channels * HALF), F32),
            jax.ShapeDtypeStruct((channels, atoms), F32),
        ),
        in_specs=[smem] + [vmem] * 5,
        out_specs=(vmem, vmem),
        scratch_shapes=[
            pltpu.VMEM((128, atoms), BF16),
            pltpu.VMEM((16, atoms), F32),
            pltpu.VMEM((leaves, channels * HALF), F32),
            pltpu.VMEM((4 * window_blocks + 4, 16, 128), F32),
            pltpu.VMEM((count, capacity, 128), jnp.int32),
            pltpu.VMEM((peers, capacity, 128), jnp.int32),
            pltpu.VMEM((peers, 2 * capacity, channels * HALF // 2), BF16),
            pltpu.VMEM((peers, 2 * capacity, channels * HALF // 2), BF16),
            pltpu.VMEM((2, 16, width), F32),
            dma((2,)),
            dma((2,)),
            dma((peers,)),
            dma((peers,)),
            dma((peers,)),
            dma((peers,)),
        ],
        compiler_params=pltpu.CompilerParams(
            vmem_limit_bytes=48 * 1024 * 1024, collective_id=0, has_side_effects=True
        ),
    )(near_index, charges[0], counts, harmonics, requests[0].T, positions)

    me = lax.axis_index(axes)
    spare = leaves + capacity * me
    index = jnp.where(m2l_slots < leaves + fetched, m2l_slots, spare).T
    index = jnp.pad(index, ((0, 0), (0, types_pad - types)))
    ops = jnp.pad(
        operators.transpose(2, 1, 0), ((0, 0), (0, HALF - terms), (0, types_pad - types))
    )
    out = pl.pallas_call(
        functools.partial(far_kernel, (leaves, slots, channels)),
        out_shape=jax.ShapeDtypeStruct((channels, atoms), F32),
        in_specs=[vmem] * 6,
        out_specs=vmem,
        scratch_shapes=[
            pltpu.VMEM((128, atoms), BF16),
            pltpu.VMEM((slots_pad // 128, channels * HALF, 128), F32),
            pltpu.VMEM((channels * leaves, HALF), F32),
        ],
        compiler_params=params,
    )(index, ops, sources, near, counts, harmonics)
    return out[None]


def solution(mesh):
    return jax.shard_map(
        per_device,
        mesh=mesh,
        in_specs=(
            P("chan", None, ("groups", "leaf", "sub")),
            P(None, ("groups", "leaf", "sub")),
            P(None, ("groups", "leaf", "sub")),
            P(),
            P(("groups", "leaf", "sub"), None),
            P(None, ("groups", "leaf", "sub")),
            P(("groups", "leaf", "sub"), None, None),
            P(None, ("groups", "leaf", "sub")),
        ),
        out_specs=P("chan", None, ("groups", "leaf", "sub")),
        check_vma=False,
    )
```

```python
import functools
import math

import jax
import jax.numpy as jnp
from jax import lax
from jax.experimental import pallas as pl
from jax.experimental.pallas import tpu as pltpu
from jax.sharding import PartitionSpec as P

HALO = 16
SOFT_SQ = 0.0625
NEAR_GAIN = 0.1
HALF = 64
NT = (((1,), (1,)), ((), ()))
F32 = jnp.float32
BF16 = jnp.bfloat16


def lane_iota(shape):
    return lax.broadcasted_iota(jnp.int32, shape, len(shape) - 1)


def chunk_mask(counts_ref, j, slots):
    shape = (8, 8 * slots)
    offset = lane_iota(shape) - slots * lax.broadcasted_iota(jnp.int32, shape, 0)
    counts = counts_ref[8 * j : 8 * j + 8, :]
    return (offset >= 0) & (offset < counts)


def fill_harmonics(harm_ref, harm2_ref):
    terms = harm_ref.shape[0]
    harm2_ref[...] = jnp.zeros_like(harm2_ref)
    harm2_ref[0:terms, :] = harm_ref[...]
    harm2_ref[HALF : HALF + terms, :] = harm_ref[...]


def compute_moments(charges_ref, counts_ref, harm2_ref, live_ref, mom_ref, leaves, slots):
    channels = charges_ref.shape[0]
    width = 8 * slots
    for j in range(leaves // 8):
        mask = chunk_mask(counts_ref, j, slots)
        q = charges_ref[:, j * width : (j + 1) * width].astype(F32)
        spread = jnp.where(mask[None], q[:, None, :], 0.0)
        live_ref[0:channels, j * width : (j + 1) * width] = jnp.sum(spread, axis=1)
        m = lax.dot_general(
            spread.reshape(channels * 8, width).astype(BF16),
            harm2_ref[:, j * width : (j + 1) * width],
            NT,
            preferred_element_type=F32,
        )
        low = lane_iota((8, 128)) < HALF
        for pair in range(channels // 2):
            mom_ref[8 * j : 8 * j + 8, 128 * pair : 128 * pair + 128] = jnp.where(
                low, m[16 * pair : 16 * pair + 8], m[16 * pair + 8 : 16 * pair + 16]
            )


def build_rolled(window, rolled_ref, first_block):
    for b in range(window.shape[1] // 128):
        block = window[:, 128 * b : 128 * b + 128]
        for r in range(4):
            rolled_ref[4 * (first_block + b) + r] = block if r == 0 else pltpu.roll(block, 32 * r, 1)


def compute_near(near_ref, rolled_ref, pos_ref, out_ref, leaves, slots, neighbours):
    groups = -(-neighbours // 4)
    last = rolled_ref.shape[0] - 1
    lane = lane_iota((16, 128))

    def body(g, carry):
        columns = pl.ds(pl.multiple_of(g * 128, 128), 128)
        targets = jnp.transpose(pos_ref[8:16, columns])
        kernels, charges = [], []
        for leaf in range(4):
            tgt = targets[32 * leaf : 32 * leaf + 32]
            tgt = [jnp.broadcast_to(tgt[:, k : k + 1], (32, 128)) for k in range(3)]
            k_parts, q_parts = [], []
            for n4 in range(groups):
                src = None
                for j in range(4):
                    n = 4 * n4 + j
                    if n < neighbours:
                        piece = rolled_ref[near_ref[n, g * 4 + leaf]]
                    else:
                        piece = rolled_ref[last]
                    src = piece if src is None else jnp.where(lane >= 32 * j, piece, src)
                squared = None
                for k in range(3):
                    d = tgt[k] - src[8 + k : 9 + k]
                    squared = d * d if squared is None else squared + d * d
                k_parts.append(lax.rsqrt(squared + SOFT_SQ).astype(BF16))
                q_parts.append(src[0:8])
            kernels.append(jnp.concatenate(k_parts, axis=1))
            charges.append(jnp.concatenate(q_parts, axis=1))
        kernels = jnp.concatenate(kernels, axis=0)
        charges = jnp.concatenate(charges, axis=0).astype(BF16)
        full = lax.dot_general(charges, kernels, NT, preferred_element_type=F32)
        lane8 = lane_iota((8, 128))
        near = full[0:8]
        for leaf in range(1, 4):
            near = jnp.where(lane8 >= 32 * leaf, full[8 * leaf : 8 * leaf + 8], near)
        out_ref[:, columns] = near
        return carry

    lax.fori_loop(0, leaves // 4, body, 0)


def gather_lanes(row, index):
    return jnp.take_along_axis(row, index, axis=1, mode="promise_in_bounds")


def compute_local(index_ref, op_ref, table_ref, tail_ref, acc_ref, leaves, channels):
    terms, _, types_pad = op_ref.shape
    blocks = table_ref.shape[0]
    batch = math.gcd(terms, 7)
    shared = tail_ref is not None
    whole = types_pad // 128 - (1 if shared else 0)
    low = lane_iota((8, 128)) < HALF
    acc_ref[...] = jnp.zeros_like(acc_ref)
    if shared:
        for pair in range(leaves // 16):
            first = index_ref[16 * pair : 16 * pair + 8, 128 * whole :]
            second = index_ref[16 * pair + 8 : 16 * pair + 16, 128 * whole :]
            tail_ref[8 * pair : 8 * pair + 8, :] = jnp.where(low, first, pltpu.roll(second, HALF, 1))

    def lookup(lines, index):
        if blocks == 1:
            return gather_lanes(lines[0], index)
        got = jnp.zeros((8, 128), F32)
        for b in range(blocks):
            got = jnp.where(index // 128 == b, gather_lanes(lines[b], index % 128), got)
        return got

    def body(step, carry):
        found = {}
        lines = {}
        for k in range(batch):
            for c in range(channels):
                lines[k, c] = [
                    jnp.broadcast_to(
                        table_ref[b, pl.ds(c * HALF + step * batch + k, 1), :], (8, 128)
                    )
                    for b in range(blocks)
                ]

        def find(k, c, l8, t):
            if t < whole:
                index = index_ref[8 * l8 : 8 * l8 + 8, 128 * t : 128 * t + 128]
                found[k, c, l8, t] = lookup(lines[k, c], index)
            elif l8 % 2 == 0:
                got = lookup(lines[k, c], tail_ref[4 * l8 : 4 * l8 + 8, :])
                found[k, c, l8, t] = jnp.where(low, got, 0.0)
                found[k, c, l8 + 1, t] = jnp.where(low, 0.0, got)

        for l8 in range(leaves // 8):
            for t in range(types_pad // 128):
                for k in range(batch):
                    for c in range(channels):
                        find(k, c, l8, t)
        parts, ops = [], []
        for k in range(batch):
            rows = [
                jnp.concatenate([found[k, c, l8, t] for t in range(types_pad // 128)], axis=1)
                for c in range(channels)
                for l8 in range(leaves // 8)
            ]
            parts.append(jnp.concatenate(rows, axis=0).astype(BF16))
            op = op_ref[step * batch + k]
            if shared:
                ops.append(op[:, : 128 * whole])
                last = op[:, 128 * whole :].astype(F32)
                ops.append((last + pltpu.roll(last, HALF, 1)).astype(BF16))
            else:
                ops.append(op)
        acc_ref[...] += lax.dot_general(
            jnp.concatenate(parts, axis=1),
            jnp.concatenate(ops, axis=1),
            NT,
            preferred_element_type=F32,
        )
        return carry

    lax.fori_loop(0, terms // batch, body, 0)


def finish(acc_ref, harm2_ref, counts_ref, near_ref, out_ref, leaves, slots, channels):
    width = 8 * slots
    for j in range(leaves // 8):
        local = jnp.concatenate(
            [acc_ref[c * leaves + 8 * j : c * leaves + 8 * j + 8] for c in range(channels)], axis=0
        ).astype(BF16)
        columns = slice(j * width, (j + 1) * width)
        far = jnp.dot(local, harm2_ref[0:HALF, columns], preferred_element_type=F32)
        mask = chunk_mask(counts_ref, j, slots)
        far = jnp.sum(jnp.where(mask[None], far.reshape(channels, 8, width), 0.0), axis=1)
        alive = jnp.sum(jnp.where(mask, 1.0, 0.0), axis=0, keepdims=True)
        out_ref[:, columns] = far + (NEAR_GAIN * alive) * near_ref[:, columns]


def exchange_kernel(
    dims, near_index_ref, charges_ref, counts_ref, harm_ref, requests_ref, positions_ref,
    sources_ref, near_ref, harm2_ref, stacked_ref, moments_ref, rolled_ref, wanted_ref, asked_ref,
    reply_ref, got_ref, halo_ref, halo_send, halo_recv, ask_send, ask_recv, reply_send, reply_recv,
):
    leaves, slots, channels, neighbours, count, subs = dims
    capacity = requests_ref.shape[0]
    atoms = leaves * slots
    width = HALO * slots
    me = lax.axis_index("leaf") * subs + lax.axis_index("sub")

    def device(rank):
        return (lax.axis_index("groups"), rank // subs, rank % subs, lax.axis_index("chan"))

    def peer(offset):
        return (me + offset) % count

    barrier = pltpu.get_barrier_semaphore()
    for d in range(1, count):
        pl.semaphore_signal(
            barrier, inc=1, device_id=device(peer(d)), device_id_type=pl.DeviceIdType.MESH
        )

    for p in range(count):
        wanted_ref[p] = jnp.broadcast_to(requests_ref[:, p : p + 1], (capacity, 128))
    fill_harmonics(harm_ref, harm2_ref)
    stacked_ref[8:16, :] = jnp.zeros((8, atoms), F32)
    stacked_ref[8:11, :] = positions_ref[...]
    compute_moments(
        charges_ref, counts_ref, harm2_ref, stacked_ref, moments_ref, leaves, slots
    )
    pl.semaphore_wait(barrier, count - 1)

    def remote(src, dst, send, recv, rank):
        return pltpu.make_async_remote_copy(
            src_ref=src, dst_ref=dst, send_sem=send, recv_sem=recv, device_id=device(rank),
            device_id_type=pl.DeviceIdType.MESH,
        )

    asks = []
    for d in range(1, count):
        copy = remote(
            wanted_ref.at[peer(d)], asked_ref.at[d - 1], ask_send.at[d - 1], ask_recv.at[d - 1],
            peer(d),
        )
        copy.start()
        asks.append(copy)
    halos = [
        remote(
            stacked_ref.at[:, pl.ds(atoms - width, width)], halo_ref.at[0], halo_send.at[0],
            halo_recv.at[0], peer(1),
        ),
        remote(
            stacked_ref.at[:, pl.ds(0, width)], halo_ref.at[1], halo_send.at[1], halo_recv.at[1],
            peer(count - 1),
        ),
    ]
    for copy in halos:
        copy.start()

    moments = moments_ref[...].astype(BF16)
    build_rolled(stacked_ref[...], rolled_ref, width // 128)
    for r in range(4):
        rolled_ref[rolled_ref.shape[0] - 4 + r] = jnp.zeros((16, 128), F32)

    lane = lane_iota((capacity, leaves))
    for copy in asks:
        copy.wait_recv()
    hot = jnp.concatenate(
        [jnp.where(asked_ref[d - 1][:, :leaves] == lane, 1.0, 0.0) for d in range(1, count)],
        axis=0,
    ).astype(BF16)
    picked = jnp.dot(hot, moments, preferred_element_type=F32)
    half = channels * HALF // 2
    replies = []
    for d in range(1, count):
        block = picked[capacity * (d - 1) : capacity * d]
        reply_ref[d - 1] = jnp.concatenate([block[:, :half], block[:, half:]], axis=0).astype(BF16)
        copy = remote(
            reply_ref.at[d - 1], got_ref.at[d - 1], reply_send.at[d - 1], reply_recv.at[d - 1],
            peer(count - d),
        )
        copy.start()
        replies.append(copy)

    for copy in halos:
        copy.wait_recv()
    build_rolled(jnp.where(me == 0, 0.0, halo_ref[0]), rolled_ref, 0)
    build_rolled(
        jnp.where(me == count - 1, 0.0, halo_ref[1]), rolled_ref, (width + atoms) // 128
    )
    compute_near(near_index_ref, rolled_ref, stacked_ref, near_ref, leaves, slots, neighbours)

    sources_ref[0:leaves, :] = moments.astype(F32)
    sources_ref[leaves:, :] = jnp.zeros((sources_ref.shape[0] - leaves, channels * HALF), F32)
    for d in range(1, count):
        replies[d - 1].wait_recv()
        block = got_ref[d - 1].astype(F32)
        rows = pl.ds(pl.multiple_of(leaves + capacity * peer(d), 8), capacity)
        sources_ref[rows, 0:half] = block[0:capacity]
        sources_ref[rows, half : 2 * half] = block[capacity : 2 * capacity]
    for copy in asks + halos + replies:
        copy.wait_send()


def far_kernel(
    dims, index_ref, op_ref, sources_ref, near_ref, counts_ref, harm_ref, out_ref, harm2_ref,
    table_ref, acc_ref, tail_ref=None,
):
    leaves, slots, channels = dims
    fill_harmonics(harm_ref, harm2_ref)
    for b in range(table_ref.shape[0]):
        block = sources_ref[128 * b : 128 * b + 128, :]
        for p in range(block.shape[1] // 128):
            table_ref[b, 128 * p : 128 * p + 128, :] = jnp.transpose(
                block[:, 128 * p : 128 * p + 128]
            )
    compute_local(index_ref, op_ref, table_ref, tail_ref, acc_ref, leaves, channels)
    finish(acc_ref, harm2_ref, counts_ref, near_ref, out_ref, leaves, slots, channels)


def per_device(
    charges, positions, harmonics, operators, leaf_atoms, near_lists, requests, m2l_slots
):
    leaves = leaf_atoms.shape[1]
    atoms = positions.shape[1]
    slots = atoms // leaves
    terms = harmonics.shape[0]
    channels = charges.shape[1]
    types = operators.shape[0]
    neighbours = near_lists.shape[0]
    fetched = requests.shape[1] * requests.shape[2]
    slots_pad = -(-(leaves + fetched) // 128) * 128
    types_pad = -(-types // 128) * 128
    counts = leaf_atoms.reshape(leaves, 1)
    vmem = pl.BlockSpec(memory_space=pltpu.VMEM)
    smem = pl.BlockSpec(memory_space=pltpu.SMEM)
    params = pltpu.CompilerParams(vmem_limit_bytes=48 * 1024 * 1024)
    axes = ("leaf", "sub")
    count = requests.shape[1]
    capacity = requests.shape[2]
    window_blocks = (leaves + 2 * HALO) * slots // 128
    width = HALO * slots
    peers = max(count - 1, 1)
    turn = (jnp.arange(neighbours, dtype=jnp.int32)[:, None] - near_lists) & 3
    near_index = (near_lists & ~3) + turn
    dma = pltpu.SemaphoreType.DMA
    sources, near = pl.pallas_call(
        functools.partial(
            exchange_kernel,
            (leaves, slots, channels, neighbours, count, lax.axis_size("sub")),
        ),
        out_shape=(
            jax.ShapeDtypeStruct((slots_pad, channels * HALF), F32),
            jax.ShapeDtypeStruct((channels, atoms), F32),
        ),
        in_specs=[smem] + [vmem] * 5,
        out_specs=(vmem, vmem),
        scratch_shapes=[
            pltpu.VMEM((128, atoms), BF16),
            pltpu.VMEM((16, atoms), F32),
            pltpu.VMEM((leaves, channels * HALF), F32),
            pltpu.VMEM((4 * window_blocks + 4, 16, 128), F32),
            pltpu.VMEM((count, capacity, 128), jnp.int32),
            pltpu.VMEM((peers, capacity, 128), jnp.int32),
            pltpu.VMEM((peers, 2 * capacity, channels * HALF // 2), BF16),
            pltpu.VMEM((peers, 2 * capacity, channels * HALF // 2), BF16),
            pltpu.VMEM((2, 16, width), F32),
            dma((2,)),
            dma((2,)),
            dma((peers,)),
            dma((peers,)),
            dma((peers,)),
            dma((peers,)),
        ],
        compiler_params=pltpu.CompilerParams(
            vmem_limit_bytes=48 * 1024 * 1024, collective_id=0, has_side_effects=True
        ),
    )(near_index, charges[0], counts, harmonics, requests[0].T, positions)

    me = lax.axis_index(axes)
    spare = leaves + capacity * me
    index = jnp.where(m2l_slots < leaves + fetched, m2l_slots, spare).T
    index = jnp.pad(index, ((0, 0), (0, types_pad - types)))
    ops = jnp.pad(
        operators.transpose(2, 1, 0), ((0, 0), (0, HALF - terms), (0, types_pad - types))
    )
    out = pl.pallas_call(
        functools.partial(far_kernel, (leaves, slots, channels)),
        out_shape=jax.ShapeDtypeStruct((channels, atoms), F32),
        in_specs=[vmem] * 6,
        out_specs=vmem,
        scratch_shapes=[
            pltpu.VMEM((128, atoms), BF16),
            pltpu.VMEM((slots_pad // 128, channels * HALF, 128), F32),
            pltpu.VMEM((channels * leaves, HALF), F32),
        ]
        + ([pltpu.VMEM((leaves // 2, 128), jnp.int32)] if 0 < types % 128 <= HALF else []),
        compiler_params=params,
    )(index, ops, sources, near, counts, harmonics)
    return out[None]


def solution(mesh):
    return jax.shard_map(
        per_device,
        mesh=mesh,
        in_specs=(
            P("chan", None, ("groups", "leaf", "sub")),
            P(None, ("groups", "leaf", "sub")),
            P(None, ("groups", "leaf", "sub")),
            P(),
            P(("groups", "leaf", "sub"), None),
            P(None, ("groups", "leaf", "sub")),
            P(("groups", "leaf", "sub"), None, None),
            P(None, ("groups", "leaf", "sub")),
        ),
        out_specs=P("chan", None, ("groups", "leaf", "sub")),
        check_vma=False,
    )
```

```python
import functools
import math

import jax
import jax.numpy as jnp
from jax import lax
from jax.experimental import pallas as pl
from jax.experimental.pallas import tpu as pltpu
from jax.sharding import PartitionSpec as P

HALO = 16
SOFT_SQ = 0.0625
NEAR_GAIN = 0.1
HALF = 64
NT = (((1,), (1,)), ((), ()))
F32 = jnp.float32
BF16 = jnp.bfloat16


def lane_iota(shape):
    return lax.broadcasted_iota(jnp.int32, shape, len(shape) - 1)


def chunk_mask(counts_ref, j, slots):
    shape = (8, 8 * slots)
    offset = lane_iota(shape) - slots * lax.broadcasted_iota(jnp.int32, shape, 0)
    counts = counts_ref[8 * j : 8 * j + 8, :]
    return (offset >= 0) & (offset < counts)


def fill_harmonics(harm_ref, harm2_ref):
    terms = harm_ref.shape[0]
    harm2_ref[...] = jnp.zeros_like(harm2_ref)
    harm2_ref[0:terms, :] = harm_ref[...]
    harm2_ref[HALF : HALF + terms, :] = harm_ref[...]


def compute_moments(charges_ref, counts_ref, harm2_ref, live_ref, mom_ref, leaves, slots):
    channels = charges_ref.shape[0]
    width = 8 * slots
    for j in range(leaves // 8):
        mask = chunk_mask(counts_ref, j, slots)
        q = charges_ref[:, j * width : (j + 1) * width].astype(F32)
        spread = jnp.where(mask[None], q[:, None, :], 0.0)
        live_ref[0:channels, j * width : (j + 1) * width] = jnp.sum(spread, axis=1)
        m = lax.dot_general(
            spread.reshape(channels * 8, width).astype(BF16),
            harm2_ref[:, j * width : (j + 1) * width],
            NT,
            preferred_element_type=F32,
        )
        low = lane_iota((8, 128)) < HALF
        for pair in range(channels // 2):
            mom_ref[8 * j : 8 * j + 8, 128 * pair : 128 * pair + 128] = jnp.where(
                low, m[16 * pair : 16 * pair + 8], m[16 * pair + 8 : 16 * pair + 16]
            )


def build_rolled(window, rolled_ref, first_block):
    for b in range(window.shape[1] // 128):
        block = window[:, 128 * b : 128 * b + 128]
        for r in range(4):
            rolled_ref[4 * (first_block + b) + r] = block if r == 0 else pltpu.roll(block, 32 * r, 1)


def compute_near(near_ref, rolled_ref, pos_ref, out_ref, leaves, slots, neighbours):
    groups = -(-neighbours // 4)
    last = rolled_ref.shape[0] - 1
    lane = lane_iota((16, 128))

    def body(g, carry):
        columns = pl.ds(pl.multiple_of(g * 128, 128), 128)
        targets = jnp.transpose(pos_ref[8:16, columns])
        kernels, charges = [], []
        for leaf in range(4):
            tgt = targets[32 * leaf : 32 * leaf + 32]
            tgt = [jnp.broadcast_to(tgt[:, k : k + 1], (32, 128)) for k in range(3)]
            k_parts, q_parts = [], []
            for n4 in range(groups):
                src = None
                for j in range(4):
                    n = 4 * n4 + j
                    if n < neighbours:
                        piece = rolled_ref[near_ref[n, g * 4 + leaf]]
                    else:
                        piece = rolled_ref[last]
                    src = piece if src is None else jnp.where(lane >= 32 * j, piece, src)
                squared = None
                for k in range(3):
                    d = tgt[k] - src[8 + k : 9 + k]
                    squared = d * d if squared is None else squared + d * d
                k_parts.append(lax.rsqrt(squared + SOFT_SQ).astype(BF16))
                q_parts.append(src[0:8])
            kernels.append(jnp.concatenate(k_parts, axis=1))
            charges.append(jnp.concatenate(q_parts, axis=1))
        kernels = jnp.concatenate(kernels, axis=0)
        charges = jnp.concatenate(charges, axis=0).astype(BF16)
        full = lax.dot_general(charges, kernels, NT, preferred_element_type=F32)
        lane8 = lane_iota((8, 128))
        near = full[0:8]
        for leaf in range(1, 4):
            near = jnp.where(lane8 >= 32 * leaf, full[8 * leaf : 8 * leaf + 8], near)
        out_ref[:, columns] = near
        return carry

    lax.fori_loop(0, leaves // 4, body, 0, unroll=2)


def gather_lanes(row, index):
    return jnp.take_along_axis(row, index, axis=1, mode="promise_in_bounds")


def compute_local(index_ref, op_ref, table_ref, tail_ref, acc_ref, leaves, channels):
    terms, _, types_pad = op_ref.shape
    blocks = table_ref.shape[0]
    batch = math.gcd(terms, 7)
    shared = tail_ref is not None
    whole = types_pad // 128 - (1 if shared else 0)
    low = lane_iota((8, 128)) < HALF
    acc_ref[...] = jnp.zeros_like(acc_ref)
    if shared:
        for pair in range(leaves // 16):
            first = index_ref[16 * pair : 16 * pair + 8, 128 * whole :]
            second = index_ref[16 * pair + 8 : 16 * pair + 16, 128 * whole :]
            tail_ref[8 * pair : 8 * pair + 8, :] = jnp.where(low, first, pltpu.roll(second, HALF, 1))

    def lookup(lines, index):
        if blocks == 1:
            return gather_lanes(lines[0], index)
        got = jnp.zeros((8, 128), F32)
        for b in range(blocks):
            got = jnp.where(index // 128 == b, gather_lanes(lines[b], index % 128), got)
        return got

    def body(step, carry):
        found = {}
        lines = {}
        for k in range(batch):
            for c in range(channels):
                lines[k, c] = [
                    jnp.broadcast_to(
                        table_ref[b, pl.ds(c * HALF + step * batch + k, 1), :], (8, 128)
                    )
                    for b in range(blocks)
                ]

        def find(k, c, l8, t):
            if t < whole:
                index = index_ref[8 * l8 : 8 * l8 + 8, 128 * t : 128 * t + 128]
                found[k, c, l8, t] = lookup(lines[k, c], index)
            elif l8 % 2 == 0:
                got = lookup(lines[k, c], tail_ref[4 * l8 : 4 * l8 + 8, :])
                found[k, c, l8, t] = jnp.where(low, got, 0.0)
                found[k, c, l8 + 1, t] = jnp.where(low, 0.0, got)

        for l8 in range(leaves // 8):
            for t in range(types_pad // 128):
                for k in range(batch):
                    for c in range(channels):
                        find(k, c, l8, t)
        parts, ops = [], []
        for k in range(batch):
            rows = [
                jnp.concatenate([found[k, c, l8, t] for t in range(types_pad // 128)], axis=1)
                for c in range(channels)
                for l8 in range(leaves // 8)
            ]
            parts.append(jnp.concatenate(rows, axis=0).astype(BF16))
            op = op_ref[step * batch + k]
            if shared:
                ops.append(op[:, : 128 * whole])
                last = op[:, 128 * whole :].astype(F32)
                ops.append((last + pltpu.roll(last, HALF, 1)).astype(BF16))
            else:
                ops.append(op)
        acc_ref[...] += lax.dot_general(
            jnp.concatenate(parts, axis=1),
            jnp.concatenate(ops, axis=1),
            NT,
            preferred_element_type=F32,
        )
        return carry

    lax.fori_loop(0, terms // batch, body, 0)


def finish(acc_ref, harm2_ref, counts_ref, near_ref, out_ref, leaves, slots, channels):
    width = 8 * slots
    for j in range(leaves // 8):
        local = jnp.concatenate(
            [acc_ref[c * leaves + 8 * j : c * leaves + 8 * j + 8] for c in range(channels)], axis=0
        ).astype(BF16)
        columns = slice(j * width, (j + 1) * width)
        far = jnp.dot(local, harm2_ref[0:HALF, columns], preferred_element_type=F32)
        mask = chunk_mask(counts_ref, j, slots)
        far = jnp.sum(jnp.where(mask[None], far.reshape(channels, 8, width), 0.0), axis=1)
        alive = jnp.sum(jnp.where(mask, 1.0, 0.0), axis=0, keepdims=True)
        out_ref[:, columns] = far + (NEAR_GAIN * alive) * near_ref[:, columns]


def exchange_kernel(
    dims, near_index_ref, charges_ref, counts_ref, harm_ref, requests_ref, positions_ref,
    sources_ref, near_ref, harm2_ref, stacked_ref, moments_ref, rolled_ref, wanted_ref, asked_ref,
    reply_ref, got_ref, halo_ref, halo_send, halo_recv, ask_send, ask_recv, reply_send, reply_recv,
):
    leaves, slots, channels, neighbours, count, subs = dims
    capacity = requests_ref.shape[0]
    atoms = leaves * slots
    width = HALO * slots
    me = lax.axis_index("leaf") * subs + lax.axis_index("sub")

    def device(rank):
        return (lax.axis_index("groups"), rank // subs, rank % subs, lax.axis_index("chan"))

    def peer(offset):
        return (me + offset) % count

    barrier = pltpu.get_barrier_semaphore()
    for d in range(1, count):
        pl.semaphore_signal(
            barrier, inc=1, device_id=device(peer(d)), device_id_type=pl.DeviceIdType.MESH
        )

    for p in range(count):
        wanted_ref[p] = jnp.broadcast_to(requests_ref[:, p : p + 1], (capacity, 128))
    fill_harmonics(harm_ref, harm2_ref)
    stacked_ref[8:16, :] = jnp.zeros((8, atoms), F32)
    stacked_ref[8:11, :] = positions_ref[...]
    compute_moments(
        charges_ref, counts_ref, harm2_ref, stacked_ref, moments_ref, leaves, slots
    )
    pl.semaphore_wait(barrier, count - 1)

    def remote(src, dst, send, recv, rank):
        return pltpu.make_async_remote_copy(
            src_ref=src, dst_ref=dst, send_sem=send, recv_sem=recv, device_id=device(rank),
            device_id_type=pl.DeviceIdType.MESH,
        )

    asks = []
    for d in range(1, count):
        copy = remote(
            wanted_ref.at[peer(d)], asked_ref.at[d - 1], ask_send.at[d - 1], ask_recv.at[d - 1],
            peer(d),
        )
        copy.start()
        asks.append(copy)
    halos = [
        remote(
            stacked_ref.at[:, pl.ds(atoms - width, width)], halo_ref.at[0], halo_send.at[0],
            halo_recv.at[0], peer(1),
        ),
        remote(
            stacked_ref.at[:, pl.ds(0, width)], halo_ref.at[1], halo_send.at[1], halo_recv.at[1],
            peer(count - 1),
        ),
    ]
    for copy in halos:
        copy.start()

    moments = moments_ref[...].astype(BF16)
    build_rolled(stacked_ref[...], rolled_ref, width // 128)
    for r in range(4):
        rolled_ref[rolled_ref.shape[0] - 4 + r] = jnp.zeros((16, 128), F32)

    lane = lane_iota((capacity, leaves))
    for copy in asks:
        copy.wait_recv()
    hot = jnp.concatenate(
        [jnp.where(asked_ref[d - 1][:, :leaves] == lane, 1.0, 0.0) for d in range(1, count)],
        axis=0,
    ).astype(BF16)
    picked = jnp.dot(hot, moments, preferred_element_type=F32)
    half = channels * HALF // 2
    replies = []
    for d in range(1, count):
        block = picked[capacity * (d - 1) : capacity * d]
        reply_ref[d - 1] = jnp.concatenate([block[:, :half], block[:, half:]], axis=0).astype(BF16)
        copy = remote(
            reply_ref.at[d - 1], got_ref.at[d - 1], reply_send.at[d - 1], reply_recv.at[d - 1],
            peer(count - d),
        )
        copy.start()
        replies.append(copy)

    for copy in halos:
        copy.wait_recv()
    build_rolled(jnp.where(me == 0, 0.0, halo_ref[0]), rolled_ref, 0)
    build_rolled(
        jnp.where(me == count - 1, 0.0, halo_ref[1]), rolled_ref, (width + atoms) // 128
    )
    compute_near(near_index_ref, rolled_ref, stacked_ref, near_ref, leaves, slots, neighbours)

    sources_ref[0:leaves, :] = moments.astype(F32)
    sources_ref[leaves:, :] = jnp.zeros((sources_ref.shape[0] - leaves, channels * HALF), F32)
    for d in range(1, count):
        replies[d - 1].wait_recv()
        block = got_ref[d - 1].astype(F32)
        rows = pl.ds(pl.multiple_of(leaves + capacity * peer(d), 8), capacity)
        sources_ref[rows, 0:half] = block[0:capacity]
        sources_ref[rows, half : 2 * half] = block[capacity : 2 * capacity]
    for copy in asks + halos + replies:
        copy.wait_send()


def far_kernel(
    dims, index_ref, op_ref, sources_ref, near_ref, counts_ref, harm_ref, out_ref, harm2_ref,
    table_ref, acc_ref, tail_ref=None,
):
    leaves, slots, channels = dims
    fill_harmonics(harm_ref, harm2_ref)
    for b in range(table_ref.shape[0]):
        block = sources_ref[128 * b : 128 * b + 128, :]
        for p in range(block.shape[1] // 128):
            table_ref[b, 128 * p : 128 * p + 128, :] = jnp.transpose(
                block[:, 128 * p : 128 * p + 128]
            )
    compute_local(index_ref, op_ref, table_ref, tail_ref, acc_ref, leaves, channels)
    finish(acc_ref, harm2_ref, counts_ref, near_ref, out_ref, leaves, slots, channels)


def per_device(
    charges, positions, harmonics, operators, leaf_atoms, near_lists, requests, m2l_slots
):
    leaves = leaf_atoms.shape[1]
    atoms = positions.shape[1]
    slots = atoms // leaves
    terms = harmonics.shape[0]
    channels = charges.shape[1]
    types = operators.shape[0]
    neighbours = near_lists.shape[0]
    fetched = requests.shape[1] * requests.shape[2]
    slots_pad = -(-(leaves + fetched) // 128) * 128
    types_pad = -(-types // 128) * 128
    counts = leaf_atoms.reshape(leaves, 1)
    vmem = pl.BlockSpec(memory_space=pltpu.VMEM)
    smem = pl.BlockSpec(memory_space=pltpu.SMEM)
    params = pltpu.CompilerParams(vmem_limit_bytes=48 * 1024 * 1024)
    axes = ("leaf", "sub")
    count = requests.shape[1]
    capacity = requests.shape[2]
    window_blocks = (leaves + 2 * HALO) * slots // 128
    width = HALO * slots
    peers = max(count - 1, 1)
    turn = (jnp.arange(neighbours, dtype=jnp.int32)[:, None] - near_lists) & 3
    near_index = (near_lists & ~3) + turn
    dma = pltpu.SemaphoreType.DMA
    sources, near = pl.pallas_call(
        functools.partial(
            exchange_kernel,
            (leaves, slots, channels, neighbours, count, lax.axis_size("sub")),
        ),
        out_shape=(
            jax.ShapeDtypeStruct((slots_pad, channels * HALF), F32),
            jax.ShapeDtypeStruct((channels, atoms), F32),
        ),
        in_specs=[smem] + [vmem] * 5,
        out_specs=(vmem, vmem),
        scratch_shapes=[
            pltpu.VMEM((128, atoms), BF16),
            pltpu.VMEM((16, atoms), F32),
            pltpu.VMEM((leaves, channels * HALF), F32),
            pltpu.VMEM((4 * window_blocks + 4, 16, 128), F32),
            pltpu.VMEM((count, capacity, 128), jnp.int32),
            pltpu.VMEM((peers, capacity, 128), jnp.int32),
            pltpu.VMEM((peers, 2 * capacity, channels * HALF // 2), BF16),
            pltpu.VMEM((peers, 2 * capacity, channels * HALF // 2), BF16),
            pltpu.VMEM((2, 16, width), F32),
            dma((2,)),
            dma((2,)),
            dma((peers,)),
            dma((peers,)),
            dma((peers,)),
            dma((peers,)),
        ],
        compiler_params=pltpu.CompilerParams(
            vmem_limit_bytes=48 * 1024 * 1024, collective_id=0, has_side_effects=True
        ),
    )(near_index, charges[0], counts, harmonics, requests[0].T, positions)

    me = lax.axis_index(axes)
    spare = leaves + capacity * me
    index = jnp.where(m2l_slots < leaves + fetched, m2l_slots, spare).T
    index = jnp.pad(index, ((0, 0), (0, types_pad - types)))
    ops = jnp.pad(
        operators.transpose(2, 1, 0), ((0, 0), (0, HALF - terms), (0, types_pad - types))
    )
    out = pl.pallas_call(
        functools.partial(far_kernel, (leaves, slots, channels)),
        out_shape=jax.ShapeDtypeStruct((channels, atoms), F32),
        in_specs=[vmem] * 6,
        out_specs=vmem,
        scratch_shapes=[
            pltpu.VMEM((128, atoms), BF16),
            pltpu.VMEM((slots_pad // 128, channels * HALF, 128), F32),
            pltpu.VMEM((channels * leaves, HALF), F32),
        ]
        + ([pltpu.VMEM((leaves // 2, 128), jnp.int32)] if 0 < types % 128 <= HALF else []),
        compiler_params=params,
    )(index, ops, sources, near, counts, harmonics)
    return out[None]


def solution(mesh):
    return jax.shard_map(
        per_device,
        mesh=mesh,
        in_specs=(
            P("chan", None, ("groups", "leaf", "sub")),
            P(None, ("groups", "leaf", "sub")),
            P(None, ("groups", "leaf", "sub")),
            P(),
            P(("groups", "leaf", "sub"), None),
            P(None, ("groups", "leaf", "sub")),
            P(("groups", "leaf", "sub"), None, None),
            P(None, ("groups", "leaf", "sub")),
        ),
        out_specs=P("chan", None, ("groups", "leaf", "sub")),
        check_vma=False,
    )
```
